256 devices in a mesh: frame: 32 (over y, z_hi, core), view: 8 (over z_lo, x).
Axes of the slice: x: 4, y: 4, z: 8 (z_hi: 4, z_lo: 2; z = z_hi * 2 + z_lo), core: 2. Of those that a mesh axis runs over, the one named last changes fastest.
Arguments:
- hidden: bfloat16 [32, 8, 128, 3072], P('frame', 'view'), may hold values from -3 to 3
- queries: bfloat16 [32, 8, 128, 3072], P('frame', 'view'), may hold values from -120 to 120
- view_keys: bfloat16 [32, 8, 128, 3072], P('frame', 'view'), may hold values from -12 to 12
- view_values: bfloat16 [32, 8, 128, 3072], P('frame', 'view'), may hold values from -12 to 12
- ref_keys: bfloat16 [32, 128, 3072], P('frame'), may hold values from -6 to 6
- ref_values: bfloat16 [32, 128, 3072], P('frame'), may hold values from -12 to 12
- temporal_query: bfloat16 [3072, 3072], P(None, 'view'), may hold values from -1.5 to 1.5
- temporal_key: bfloat16 [3072, 3072], P(None, 'view'), may hold values from -1.5 to 1.5
- temporal_value: bfloat16 [3072, 3072], P(None, 'view'), may hold values from -0.109375 to 0.109375
Outputs:
- mixed: bfloat16 [32, 8, 128, 3072], P('frame', 'view')
- temporal_out: bfloat16 [32, 8, 128, 3072], P('frame', None, None, 'view')
The draws below stay inside these ranges and needn't reach their ends.
All inputs are finite; a program needn't handle non-finite values.
Results may differ from the reference program's by a relative error of at most 0.035.
Values may be sent and summed in bfloat16 or wider, within the bound.
A program may use at most 128 MiB of HBM per device.

```python
import jax
import jax.numpy as jnp
from jax import lax

HEADS = 24
HEAD_SIZE = 128
PIX = 128
D = 3072
VIEWS = 8
FRAMES = 32


def shared_attention(key):
    first, second = jax.random.split(key, 2)
    shape = (FRAMES, VIEWS, PIX, HEADS * HEAD_SIZE)
    keys_drawn = jax.random.normal(first, shape, jnp.float32)
    queries_drawn = 2.0 * jax.random.normal(second, shape, jnp.float32)
    queries_drawn = jnp.clip(queries_drawn, -120.0, 120.0)
    keys_drawn = jnp.clip(keys_drawn, -12.0, 12.0)
    return (queries_drawn, keys_drawn)


def draw_queries(key, part):
    return shared_attention(key)[0].astype(jnp.bfloat16)


def draw_view_keys(key, part):
    return shared_attention(key)[1].astype(jnp.bfloat16)


def shared_temporal(key):
    first, second = jax.random.split(jax.random.fold_in(key, 7), 2)
    width = HEADS * HEAD_SIZE
    key_weight = jax.random.normal(first, (width, width), jnp.float32) * width ** (-0.5)
    query_weight = jax.random.normal(second, (width, width), jnp.float32) * width ** (-0.5)
    return (jnp.clip(query_weight, -1.5, 1.5), jnp.clip(key_weight, -1.5, 1.5))


def draw_temporal_query(key, part):
    return shared_temporal(key)[0].astype(jnp.bfloat16)


def draw_temporal_key(key, part):
    return shared_temporal(key)[1].astype(jnp.bfloat16)


def block_levels(key, dims, cuts, smallest, high):
    def one(axis_at, parts):
        heights = jax.random.uniform(jax.random.fold_in(jax.random.fold_in(key, 6), axis_at), (parts,), jnp.float32, smallest / len(cuts), high / len(cuts))
        return jnp.repeat(jnp.exp(heights), dims[axis_at] // parts).reshape((-1,) + (1,) * (len(dims) - axis_at - 1))

    level = one(*cuts[0])
    for cut in cuts[1:]:
        level = level * one(*cut)
    return level


def centred(stream_key, extent, scale, reach, shards=(), held_as=jnp.bfloat16):
    loudness = block_levels(stream_key, extent, shards, -0.22, 0.18) if shards else 1.0
    entries = jax.random.normal(stream_key, extent, jnp.float32) * scale * loudness
    return jnp.minimum(jnp.maximum(entries, -reach), reach).astype(held_as)


def setup_inputs(seed: int = 0) -> dict:
    arg_keys = jax.random.split(jax.random.key(seed), 10)
    hidden = centred(arg_keys[0], (FRAMES, VIEWS, PIX, D), 0.5, 3.0, ((0, 32), (1, 8)))
    queries = draw_queries(jax.random.fold_in(arg_keys[9], 71), 0)
    view_keys = draw_view_keys(jax.random.fold_in(arg_keys[9], 71), 0)
    view_values = centred(arg_keys[3], (FRAMES, VIEWS, PIX, D), 2.0, 12.0, ((0, 32), (1, 8)))
    ref_keys = centred(arg_keys[4], (FRAMES, PIX, D), 1.0, 6.0, ((0, 32),))
    ref_values = centred(arg_keys[5], (FRAMES, PIX, D), 2.0, 12.0, ((0, 32),))
    temporal_query = draw_temporal_query(jax.random.fold_in(arg_keys[9], 71), 0)
    temporal_key = draw_temporal_key(jax.random.fold_in(arg_keys[9], 71), 0)
    temporal_value = centred(arg_keys[8], (D, D), D ** -0.5, 0.109375, ((1, 8),))
    return dict(hidden=hidden, queries=queries, view_keys=view_keys, view_values=view_values, ref_keys=ref_keys, ref_values=ref_values, temporal_query=temporal_query, temporal_key=temporal_key, temporal_value=temporal_value)


def view_frame(items):
    frame_queries, frame_keys, frame_values = items
    rows = frame_queries.shape[0] * frame_queries.shape[1]
    query_heads = frame_queries.reshape(rows, HEADS, HEAD_SIZE).astype(jnp.float32)
    key_heads = frame_keys.reshape(-1, HEADS, HEAD_SIZE).astype(jnp.float32)
    value_heads = frame_values.reshape(-1, HEADS, HEAD_SIZE).astype(jnp.float32)
    scores = jnp.einsum('qhd,khd->hqk', query_heads, key_heads) * (HEAD_SIZE ** -0.5)
    weights = jax.nn.softmax(scores, axis=-1).astype(jnp.bfloat16)
    attn = jnp.einsum('hqk,khd->qhd', weights.astype(jnp.float32), value_heads)
    return attn.reshape(frame_queries.shape)


def reference(hidden, queries, view_keys, view_values, ref_keys, ref_values, temporal_query, temporal_key, temporal_value):
    frames, views, pix, width = hidden.shape
    all_keys = jnp.concatenate([view_keys.reshape(frames, views * pix, width), ref_keys], axis=1)
    all_values = jnp.concatenate([view_values.reshape(frames, views * pix, width), ref_values], axis=1)
    view_attn = lax.map(view_frame, (queries, all_keys, all_values))
    mixed = (hidden.astype(jnp.float32) + view_attn).astype(jnp.bfloat16)
    flat = mixed.reshape(-1, width)
    shape = (frames, views * pix, HEADS, HEAD_SIZE)
    tq = jnp.dot(flat, temporal_query, preferred_element_type=jnp.float32).astype(jnp.bfloat16).reshape(shape)
    tk = jnp.dot(flat, temporal_key, preferred_element_type=jnp.float32).astype(jnp.bfloat16).reshape(shape)
    tv = jnp.dot(flat, temporal_value, preferred_element_type=jnp.float32).astype(jnp.bfloat16).reshape(shape)
    scores = jnp.einsum('fmhd,gmhd->mhfg', tq.astype(jnp.float32), tk.astype(jnp.float32)) * (HEAD_SIZE ** -0.5)
    weights = jax.nn.softmax(scores, axis=-1).astype(jnp.bfloat16)
    out = jnp.einsum('mhfg,gmhd->fmhd', weights.astype(jnp.float32), tv.astype(jnp.float32))
    temporal_out = out.reshape(frames, views, pix, width).astype(jnp.bfloat16)
    return mixed, temporal_out
```

```python
import functools

import jax
import jax.numpy as jnp
from jax import lax
from jax.experimental import pallas as pl
from jax.experimental.pallas import tpu as pltpu
from jax.sharding import PartitionSpec as P

MESH = pl.DeviceIdType.MESH
BF16 = jnp.bfloat16
F32 = jnp.float32
SCALE = 128 ** (-0.5) * 1.4426950408889634


def softmax_parts(scores, values):
    top = jnp.max(scores, axis=-1, keepdims=True)
    weights = jnp.exp2((scores - top) * SCALE).astype(BF16)
    product = jnp.dot(weights, values, preferred_element_type=F32)
    return product[:, :128] / product[:, 128:]


def bytes_wait(ref, sem):
    pltpu.make_async_copy(ref, ref, sem).wait()


def kernel(
    hid, qry, key, val, rkey, rval, wq, wk, wv,
    mixed_out, time_out,
    qbuf, kbuf, vbuf, hbuf, abuf, mbuf, xall, wbuf, tqkv, obuf,
    p1_send, p1_recv, loc, h_send, h_recv, wl_sem, w_send, w1_recv, w2_recv, w3_recv,
    p2_send, p2_recv, p3_send, p3_recv, mb_send, mb_recv, p5_send, p5_recv, own_sem,
):
    f = lax.axis_index("frame")
    v = lax.axis_index("view")
    y, zh, c = f // 8, (f // 2) % 4, f % 2
    zl, x = v // 4, v % 4
    z = zh * 2 + zl

    def device(y_, z_, c_, x_):
        return (y_ * 8 + (z_ // 2) * 2 + c_, (z_ % 2) * 4 + x_)

    def column(part, width=384):
        return pl.ds(pl.multiple_of(part * width, width), width)

    def remote(src, dst, send, recv, target):
        return pltpu.make_async_remote_copy(
            src_ref=src, dst_ref=dst, send_sem=send, recv_sem=recv, device_id=target, device_id_type=MESH
        )

    barrier = pltpu.get_barrier_semaphore()

    def greet_same_x(i, _):
        target = device((y + i // 16) % 4, (z + (i // 2) % 8) % 8, (c + i % 2) % 2, x)
        pl.semaphore_signal(barrier, inc=1, device_id=target, device_id_type=MESH)
        return 0

    lax.fori_loop(1, 64, greet_same_x, 0)

    def greet_view(i, _):
        target = (f, (i // 3) * 4 + (x + 1 + i % 3) % 4)
        pl.semaphore_signal(barrier, inc=1, device_id=target, device_id_type=MESH)
        return 0

    lax.fori_loop(0, 6, greet_view, 0)

    def local_heads(h, _):
        cols = pl.ds(pl.multiple_of(v * 384 + h * 128, 128), 128)
        pltpu.make_async_copy(qry.at[:, cols], qbuf.at[h, v], loc.at[h, 0]).start()
        pltpu.make_async_copy(key.at[:, cols], kbuf.at[h, v], loc.at[h, 1]).start()
        pltpu.make_async_copy(rkey.at[:, cols], kbuf.at[h, 8], loc.at[h, 1]).start()
        pltpu.make_async_copy(val.at[:, cols], vbuf.at[h, v, :, 0:128], loc.at[h, 2]).start()
        pltpu.make_async_copy(rval.at[:, cols], vbuf.at[h, 8, :, 0:128], loc.at[h, 2]).start()
        return 0

    lax.fori_loop(0, 3, local_heads, 0)
    pltpu.make_async_copy(hid.at[:, column(v)], hbuf.at[v], own_sem.at[0]).start()

    def load_weights(i, _):
        rows = column(i)
        place = pl.ds(pl.multiple_of((i // 4) * 384, 384), 384)
        for a, w in enumerate((wq, wk, wv)):
            pltpu.make_async_copy(
                w.at[rows], wbuf.at[0, i % 4, place, a * 384 : (a + 1) * 384], wl_sem.at[0]
            ).start()
        return 0

    pl.semaphore_wait(barrier, 69)

    def send_heads(h, _):
        def to(i, _):
            w = (v + i) % 8
            cols = pl.ds(pl.multiple_of(w * 384 + h * 128, 128), 128)
            remote(key.at[:, cols], kbuf.at[h, v], p1_send.at[1], p1_recv.at[h, 1], (f, w)).start()
            remote(qry.at[:, cols], qbuf.at[h, v], p1_send.at[0], p1_recv.at[h, 0], (f, w)).start()
            remote(val.at[:, cols], vbuf.at[h, v, :, 0:128], p1_send.at[2], p1_recv.at[h, 2], (f, w)).start()
            return 0

        return lax.fori_loop(1, 8, to, 0)

    lax.fori_loop(0, 3, send_heads, 0)

    def send_hidden(i, _):
        w = (v + i) % 8
        remote(hid.at[:, column(w)], hbuf.at[v], h_send.at[0], h_recv.at[0], (f, w)).start()
        return 0

    lax.fori_loop(1, 8, send_hidden, 0)

    part = c * 4 + y
    z_far = (z + 7 + 2 * zl) % 8

    def part_place(c_, y_):
        return wbuf.at[1, y_, pl.ds(pl.multiple_of(c_ * 384, 384), 384)]

    for a, w in enumerate((wq, wk, wv)):
        remote(
            w.at[column(part)],
            wbuf.at[1, y, pl.ds(pl.multiple_of(c * 384, 384), 384), a * 384 : (a + 1) * 384],
            w_send.at[0],
            w1_recv.at[0],
            device(y, z_far, c, x),
        ).start()
    lax.fori_loop(0, 8, load_weights, 0)

    vbuf[:, :, :, 128:256] = jnp.ones((3, 9, 128, 128), BF16)

    def view_head(h, _):
        bytes_wait(kbuf.at[h, 0:2], loc.at[h, 1])
        bytes_wait(qbuf.at[h, 0:1], loc.at[h, 0])
        bytes_wait(kbuf.at[h, 0:2], loc.at[h, 2])
        bytes_wait(qbuf.at[h, 0:7], p1_recv.at[h, 0])
        bytes_wait(kbuf.at[h, 0:7], p1_recv.at[h, 1])
        bytes_wait(kbuf.at[h, 0:7], p1_recv.at[h, 2])
        keys = kbuf[h].reshape(1152, 128)
        values = vbuf[h].reshape(1152, 256)

        def rows(r, _):
            q = qbuf[h, pl.ds(r * 2, 2)].reshape(256, 128)
            scores = lax.dot_general(q, keys, (((1,), (1,)), ((), ())), preferred_element_type=F32)
            abuf[h, pl.ds(r * 2, 2)] = softmax_parts(scores, values).reshape(2, 128, 128)
            return 0

        return lax.fori_loop(0, 4, rows, 0)

    lax.fori_loop(0, 2, view_head, 0)

    bytes_wait(part_place(c, y), w1_recv.at[0])
    for i in (1, 3, 2):
        remote(part_place(c, y), part_place(c, y), w_send.at[1], w2_recv.at[0], device((y + i) % 4, z, c, x)).start()

    lax.fori_loop(2, 3, view_head, 0)

    bytes_wait(hbuf.at[0:1], own_sem.at[0])
    bytes_wait(hbuf.at[0:7], h_recv.at[0])

    def tokens_out(d, _):
        y_to = (y + d) % 4
        views = pl.ds(y_to * 2, 2)
        block = hbuf[views].astype(F32) + jnp.concatenate([abuf[h, views] for h in range(3)], axis=-1)
        mbuf[pl.ds(pl.multiple_of(y_to * 256, 256), 256)] = block.reshape(256, 384).astype(BF16)

        def to(j, _):
            z_to, c_to = (z + j // 2) % 8, (c + j % 2) % 2
            group = y_to * 16 + z_to * 2 + c_to
            remote(
                mbuf.at[pl.ds(pl.multiple_of(group * 16, 16), 16)],
                xall.at[x, pl.ds(pl.multiple_of(f * 16, 16), 16), column(zl)],
                p2_send.at[0],
                p2_recv.at[d],
                device(y_to, z_to, c_to, x),
            ).start()
            return 0

        return lax.fori_loop(jnp.where(d == 0, 1, 0), 16, to, 0)

    lax.fori_loop(0, 4, tokens_out, 0)
    mine = pltpu.make_async_copy(
        mbuf.at[pl.ds(pl.multiple_of((y * 16 + z * 2 + c) * 16, 16), 16)],
        xall.at[x, pl.ds(pl.multiple_of(f * 16, 16), 16), column(zl)],
        own_sem.at[1],
    )
    mine.start()
    mine_mixed = pltpu.make_async_copy(
        mbuf.at[pl.ds(pl.multiple_of(v * 128, 128), 128)], mixed_out.at[:, column(v)], own_sem.at[2]
    )
    mine_mixed.start()

    def send_mixed(i, _):
        w = (v + i) % 8
        remote(
            mbuf.at[pl.ds(pl.multiple_of(w * 128, 128), 128)],
            mixed_out.at[:, column(v)],
            mb_send.at[0],
            mb_recv.at[0],
            (f, w),
        ).start()
        return 0

    lax.fori_loop(1, 8, send_mixed, 0)

    def gather(d):
        y_from = (y + 4 - d) % 4
        rows = pl.ds(pl.multiple_of(y_from * 128, 128), 128)
        for i in (1, 3, 2):
            remote(
                xall.at[x, rows], xall.at[x, rows], p3_send.at[0], p3_recv.at[i], (f, zl * 4 + (x + i) % 4)
            ).start()

    mine.wait()
    bytes_wait(mbuf.at[0:240], p2_recv.at[0])
    gather(0)

    def gather_next(d, _):
        bytes_wait(mbuf.at[0:256], p2_recv.at[d])
        gather(d)
        return 0

    lax.fori_loop(1, 4, gather_next, 0)

    bytes_wait(wbuf.at[1, 0:3, 0:384], w2_recv.at[0])
    for i in range(4):
        remote(part_place(c, i), part_place(c, i), w_send.at[2], w3_recv.at[0], device(y, z, 1 - c, x)).start()

    bytes_wait(wbuf.at[0], wl_sem.at[0])
    for i in (1, 3, 2):
        bytes_wait(xall.at[0], p3_recv.at[i])

    row = lax.broadcasted_iota(jnp.int32, (1, 16, 512), 1)
    col = lax.broadcasted_iota(jnp.int32, (1, 16, 512), 2)
    same = row == col % 16
    tqkv[2, :, :, 128:256] = jnp.ones((3, 512, 128), BF16)

    def project(s):
        def rows(r, _):
            at = pl.ds(pl.multiple_of(r * 256, 256), 256)
            total = jnp.dot(xall[0, at], wbuf[s, 0], preferred_element_type=F32)
            for b in range(1, 4):
                total += jnp.dot(xall[b, at], wbuf[s, b], preferred_element_type=F32)
            total = total.astype(BF16)
            for a in range(3):
                for h in range(3):
                    start = a * 384 + h * 128
                    tqkv[a, h, at, 0:128] = total[:, start : start + 128]
            return 0

        lax.fori_loop(0, 2, rows, 0)

    def time_heads(s):
        for h in range(3):
            q, k = tqkv[0, h, :, 0:128], tqkv[1, h, :, 0:128]
            scores = lax.dot_general(q, k, (((1,), (1,)), ((), ())), preferred_element_type=F32)
            scores = jnp.where(same, scores.reshape(32, 16, 512), -jnp.inf).reshape(512, 512)
            obuf[s, :, h * 128 : (h + 1) * 128] = softmax_parts(scores, tqkv[2, h]).astype(BF16)

    group_rows = pl.ds(pl.multiple_of((y * 16 + z * 2 + c) * 16, 16), 16)

    def half(s, _):
        @pl.when(s == 1)
        def _():
            bytes_wait(wbuf.at[1, :, 0:384], w3_recv.at[0])

        project(s)
        time_heads(s)
        zl_to = (zl + s) % 2

        def to(i, _):
            f_to = (f + i) % 32
            remote(
                obuf.at[s, pl.ds(pl.multiple_of(f_to * 16, 16), 16)],
                time_out.at[group_rows],
                p5_send.at[0],
                p5_recv.at[0],
                (f_to, zl_to * 4 + x),
            ).start()
            return 0

        return lax.fori_loop(jnp.where(s == 0, 1, 0), 32, to, 0)

    lax.fori_loop(0, 2, half, 0)
    mine_out = pltpu.make_async_copy(
        obuf.at[0, pl.ds(pl.multiple_of(f * 16, 16), 16)], time_out.at[group_rows], own_sem.at[3]
    )
    mine_out.start()

    mine_mixed.wait()
    mine_out.wait()
    bytes_wait(hbuf.at[0:7], mb_recv.at[0])
    bytes_wait(mbuf.at[0:1008], p5_recv.at[0])
    for a in range(3):
        bytes_wait(kbuf.at[:, 0:7], p1_send.at[a])
    bytes_wait(hbuf.at[0:7], h_send.at[0])
    bytes_wait(wbuf.at[1, 0, 0:384], w_send.at[0])
    bytes_wait(wbuf.at[1, 0:3, 0:384], w_send.at[1])
    bytes_wait(wbuf.at[1, :, 0:384], w_send.at[2])
    bytes_wait(mbuf.at[0:1008], p2_send.at[0])
    bytes_wait(xall.at[0:3], p3_send.at[0])
    bytes_wait(hbuf.at[0:7], mb_send.at[0])
    bytes_wait(mbuf.at[0:1008], p5_send.at[0])


def on_device(hidden, queries, view_keys, view_values, ref_keys, ref_values, temporal_query, temporal_key, temporal_value):
    flat = [a.reshape(128, 3072) for a in (hidden, queries, view_keys, view_values, ref_keys, ref_values)]
    dma = pltpu.SemaphoreType.DMA
    mixed, out = pl.pallas_call(
        kernel,
        out_shape=(jax.ShapeDtypeStruct((128, 3072), BF16), jax.ShapeDtypeStruct((1024, 384), BF16)),
        in_specs=[pl.BlockSpec(memory_space=pl.ANY)] * 9,
        out_specs=(pl.BlockSpec(memory_space=pl.ANY), pl.BlockSpec(memory_space=pl.ANY)),
        scratch_shapes=[
            pltpu.VMEM((3, 8, 128, 128), BF16),
            pltpu.VMEM((3, 9, 128, 128), BF16),
            pltpu.VMEM((3, 9, 128, 256), BF16),
            pltpu.VMEM((8, 128, 384), BF16),
            pltpu.VMEM((3, 8, 128, 128), F32),
            pltpu.VMEM((1024, 384), BF16),
            pltpu.VMEM((4, 512, 768), BF16),
            pltpu.VMEM((2, 4, 768, 1152), BF16),
            pltpu.VMEM((3, 3, 512, 256), BF16),
            pltpu.VMEM((2, 512, 384), BF16),
            dma((3,)), dma((3, 3)), dma((3, 3)), dma((1,)), dma((1,)), dma((1,)), dma((3,)), dma((1,)), dma((1,)), dma((1,)),
            dma((1,)), dma((4,)), dma((1,)), dma((4,)), dma((1,)), dma((1,)), dma((1,)), dma((1,)), dma((4,)),
        ],
        compiler_params=pltpu.CompilerParams(
            collective_id=0, has_side_effects=True, vmem_limit_bytes=58 << 20
        ),
    )(*flat, temporal_query, temporal_key, temporal_value)
    return mixed.reshape(1, 1, 128, 3072), out.reshape(1, 8, 128, 384)


def solution(mesh):
    placed = (
        P("frame", "view", None, None),
        P("frame", "view", None, None),
        P("frame", "view", None, None),
        P("frame", "view", None, None),
        P("frame", None, None),
        P("frame", None, None),
        P(None, "view"),
        P(None, "view"),
        P(None, "view"),
    )
    return jax.shard_map(
        on_device,
        mesh=mesh,
        in_specs=placed,
        out_specs=(P("frame", "view", None, None), P("frame", None, None, "view")),
        check_vma=False,
    )
```

```python
import functools

import jax
import jax.numpy as jnp
from jax import lax
from jax.experimental import pallas as pl
from jax.experimental.pallas import tpu as pltpu
from jax.sharding import PartitionSpec as P

MESH = pl.DeviceIdType.MESH
BF16 = jnp.bfloat16
F32 = jnp.float32
SCALE = 128 ** (-0.5) * 1.4426950408889634


def softmax_parts(scores, values):
    top = jnp.max(scores, axis=-1, keepdims=True)
    weights = jnp.exp2((scores - top) * SCALE).astype(BF16)
    product = jnp.dot(weights, values, preferred_element_type=F32)
    return product[:, :128] / product[:, 128:]


def bytes_wait(ref, sem):
    pltpu.make_async_copy(ref, ref, sem).wait()


def kernel(
    hid, qry, key, val, rkey, rval, wq, wk, wv,
    mixed_out, time_out,
    qbuf, kbuf, vbuf, hbuf, abuf, mbuf, xall, wbuf, tqkv, obuf,
    p1_send, p1_recv, loc, h_send, h_recv, wl_sem, w_send, w1_recv, w2_recv, w3_recv,
    p2_send, p2_recv, p3_send, p3_recv, mb_send, mb_recv, p5_send, p5_recv, own_sem,
    core_in, plane_in,
):
    f = lax.axis_index("frame")
    v = lax.axis_index("view")
    y, zh, c = f // 8, (f // 2) % 4, f % 2
    zl, x = v // 4, v % 4
    z = zh * 2 + zl
    z_skip = 1 + 6 * zl

    def device(y_, z_, c_, x_):
        return (y_ * 8 + (z_ // 2) * 2 + c_, (z_ % 2) * 4 + x_)

    def column(part, width=384):
        return pl.ds(pl.multiple_of(part * width, width), width)

    def remote(src, dst, send, recv, target):
        return pltpu.make_async_remote_copy(
            src_ref=src, dst_ref=dst, send_sem=send, recv_sem=recv, device_id=target, device_id_type=MESH
        )

    barrier = pltpu.get_barrier_semaphore()

    def greet(target, sem=barrier):
        pl.semaphore_signal(sem, inc=1, device_id=target, device_id_type=MESH)

    def greet_view(i, _):
        greet((f, (v + i) % 8))
        return 0

    def greet_z(i, _):
        greet(device(y, (z + i) % 8, c, x))
        return 0

    def greet_y(i, _):
        greet(device((y + i) % 4, z, c, x))
        return 0

    lax.fori_loop(1, 8, greet_view, 0)
    lax.fori_loop(1, 7, lambda i, _: greet_z(i + jnp.where(i >= z_skip, 1, 0), _), 0)
    lax.fori_loop(1, 4, greet_y, 0)
    greet(device(y, z, 1 - c, x))

    def local_heads(h, _):
        cols = pl.ds(pl.multiple_of(v * 384 + h * 128, 128), 128)
        pltpu.make_async_copy(qry.at[:, cols], qbuf.at[h, v], loc.at[h, 0]).start()
        pltpu.make_async_copy(key.at[:, cols], kbuf.at[h, v], loc.at[h, 1]).start()
        pltpu.make_async_copy(rkey.at[:, cols], kbuf.at[h, 8], loc.at[h, 1]).start()
        pltpu.make_async_copy(val.at[:, cols], vbuf.at[h, v, :, 0:128], loc.at[h, 2]).start()
        pltpu.make_async_copy(rval.at[:, cols], vbuf.at[h, 8, :, 0:128], loc.at[h, 2]).start()
        return 0

    lax.fori_loop(0, 3, local_heads, 0)
    pltpu.make_async_copy(hid.at[:, column(v)], hbuf.at[v], own_sem.at[0]).start()

    def load_weights(i, _):
        rows = column(i)
        place = pl.ds(pl.multiple_of((i // 4) * 384, 384), 384)
        for a, w in enumerate((wq, wk, wv)):
            pltpu.make_async_copy(
                w.at[rows], wbuf.at[0, i % 4, place, a * 384 : (a + 1) * 384], wl_sem.at[0]
            ).start()
        return 0

    pl.semaphore_wait(barrier, 17)

    z_far = (z + 7 + 2 * zl) % 8

    def part_rows(odd, p):
        block = odd * 4 + p
        return column(block), wbuf.at[1, p, pl.ds(pl.multiple_of(odd * 384, 384), 384)]

    odd = y % 2

    def bring(n):
        rows, place = part_rows(odd, 2 * n + c)
        for a, w in enumerate((wq, wk, wv)):
            remote(
                w.at[rows],
                place.at[:, a * 384 : (a + 1) * 384],
                w_send.at[0],
                w1_recv.at[n],
                device(y, z_far, c, x),
            ).start()

    def part_wait(sem):
        bytes_wait(wbuf.at[1, 0, 0:384], sem)

    def to_y(n):
        _, place = part_rows(odd, 2 * n + c)
        remote(place, place, w_send.at[1], w2_recv.at[n], device((y + 1 + 2 * n) % 4, z, c, x)).start()

    def to_core(set_odd, n):
        _, place = part_rows(set_odd, 2 * n + c)
        remote(place, place, w_send.at[2], w3_recv.at[0], device(y, z, 1 - c, x)).start()

    bring(0)

    def send_heads(h, _):
        def to(i, _):
            w = (v + i) % 8
            cols = pl.ds(pl.multiple_of(w * 384 + h * 128, 128), 128)
            remote(key.at[:, cols], kbuf.at[h, v], p1_send.at[1], p1_recv.at[h, 1], (f, w)).start()
            remote(qry.at[:, cols], qbuf.at[h, v], p1_send.at[0], p1_recv.at[h, 0], (f, w)).start()
            remote(val.at[:, cols], vbuf.at[h, v, :, 0:128], p1_send.at[2], p1_recv.at[h, 2], (f, w)).start()
            return 0

        return lax.fori_loop(1, 8, to, 0)

    lax.fori_loop(0, 3, send_heads, 0)

    def send_hidden(i, _):
        w = (v + i) % 8
        remote(hid.at[:, column(w)], hbuf.at[v], h_send.at[0], h_recv.at[0], (f, w)).start()
        return 0

    lax.fori_loop(1, 8, send_hidden, 0)

    greet(device(y, z, 1 - c, x), core_in.at[0])
    lax.fori_loop(0, 8, load_weights, 0)

    vbuf[:, :, :, 128:256] = jnp.ones((3, 9, 128, 128), BF16)
    tqkv[:, 2, :, :, 128:256] = jnp.ones((2, 3, 512, 128), BF16)

    def view_head(h, _):
        bytes_wait(kbuf.at[h, 0:2], loc.at[h, 1])
        bytes_wait(qbuf.at[h, 0:1], loc.at[h, 0])
        bytes_wait(kbuf.at[h, 0:2], loc.at[h, 2])
        bytes_wait(qbuf.at[h, 0:7], p1_recv.at[h, 0])
        bytes_wait(kbuf.at[h, 0:7], p1_recv.at[h, 1])
        bytes_wait(kbuf.at[h, 0:7], p1_recv.at[h, 2])
        keys = kbuf[h].reshape(1152, 128)
        values = vbuf[h].reshape(1152, 256)

        def rows(r, _):
            q = qbuf[h, pl.ds(r * 2, 2)].reshape(256, 128)
            scores = lax.dot_general(q, keys, (((1,), (1,)), ((), ())), preferred_element_type=F32)
            abuf[h, pl.ds(r * 2, 2)] = softmax_parts(scores, values).reshape(2, 128, 128)
            return 0

        return lax.fori_loop(0, 4, rows, 0)

    lax.fori_loop(0, 1, view_head, 0)
    bring(1)
    pl.semaphore_wait(core_in.at[0], 1)
    for i in range(1, 4):
        greet(device((y + i) % 4, z, c, x), plane_in.at[0])
    lax.fori_loop(1, 2, view_head, 0)
    part_wait(w1_recv.at[0])
    to_y(0)
    to_core(odd, 0)
    lax.fori_loop(2, 3, view_head, 0)
    pl.semaphore_wait(plane_in.at[0], 3)

    bytes_wait(hbuf.at[0:1], own_sem.at[0])
    bytes_wait(hbuf.at[0:7], h_recv.at[0])

    def tokens_out(n, _):
        c_to, d = n // 4, n % 4
        y_to = (y + d) % 4

        @pl.when(c_to == 0)
        def _():
            views = pl.ds(y_to * 2, 2)
            block = hbuf[views].astype(F32) + jnp.concatenate([abuf[h, views] for h in range(3)], axis=-1)
            mbuf[pl.ds(pl.multiple_of(y_to * 256, 256), 256)] = block.reshape(256, 384).astype(BF16)

        def to(j, _):
            z_to = (z + j) % 8
            group = y_to * 16 + z_to * 2 + c_to
            remote(
                mbuf.at[pl.ds(pl.multiple_of(group * 16, 16), 16)],
                xall.at[x, pl.ds(pl.multiple_of(d * 128 + (f % 8) * 16, 16), 16), column(zl)],
                p2_send.at[0],
                p2_recv.at[d],
                device(y_to, z_to, c_to, x),
            ).start()
            return 0

        return lax.fori_loop(jnp.where((d == 0) & (c_to == c), 1, 0), 8, to, 0)

    lax.fori_loop(0, 8, tokens_out, 0)
    mine = pltpu.make_async_copy(
        mbuf.at[pl.ds(pl.multiple_of((y * 16 + z * 2 + c) * 16, 16), 16)],
        xall.at[x, pl.ds(pl.multiple_of((f % 8) * 16, 16), 16), column(zl)],
        own_sem.at[1],
    )
    mine.start()
    mine_mixed = pltpu.make_async_copy(
        mbuf.at[pl.ds(pl.multiple_of(v * 128, 128), 128)], mixed_out.at[:, column(v)], own_sem.at[2]
    )
    mine_mixed.start()

    def send_mixed(i, _):
        w = (zl + i // 4) % 2 * 4 + (x + i % 4) % 4
        remote(
            mbuf.at[pl.ds(pl.multiple_of(w * 128, 128), 128)],
            mixed_out.at[:, column(v)],
            mb_send.at[0],
            mb_recv.at[0],
            (f, w),
        ).start()
        return 0

    lax.fori_loop(1, 4, send_mixed, 0)
    part_wait(w1_recv.at[1])
    to_y(1)
    to_core(odd, 1)

    def x_device(i):
        return (f, zl * 4 + (x + i) % 4)

    def direct(d):
        rows = pl.ds(pl.multiple_of(d * 128, 128), 128)
        remote(xall.at[x, rows], xall.at[x, rows], p3_send.at[0], p3_recv.at[0, d], x_device(1)).start()
        remote(xall.at[x, rows], xall.at[x, rows], p3_send.at[0], p3_recv.at[1, d], x_device(3)).start()

    def forward(d):
        for n in range(2):
            bytes_wait(xall.at[0, 0:128], p3_recv.at[n, d])
            rows = pl.ds(pl.multiple_of(d * 128 + n * 64, 64), 64)
            block = xall.at[(x + 3 + 2 * n) % 4, rows]
            remote(block, block, p3_send.at[1], p3_recv.at[2, d], x_device(1 + 2 * n)).start()

    def gather(d, _):
        bytes_wait(mbuf.at[0:256], p2_recv.at[d])
        direct(d)
        forward(d - 1)
        return 0

    mine.wait()
    bytes_wait(mbuf.at[0:240], p2_recv.at[0])
    direct(0)
    lax.fori_loop(1, 2, gather, 0)
    part_wait(w2_recv.at[0])
    to_core(1 - odd, 0)
    lax.fori_loop(2, 4, gather, 0)
    bytes_wait(wbuf.at[0], wl_sem.at[0])

    row = lax.broadcasted_iota(jnp.int32, (1, 16, 512), 1)
    col = lax.broadcasted_iota(jnp.int32, (1, 16, 512), 2)
    same = row == col % 16

    def project(s, r):
        at = pl.ds(pl.multiple_of(r * 256, 256), 256)
        total = jnp.dot(xall[0, at], wbuf[s, 0], preferred_element_type=F32)
        for b in range(1, 4):
            total += jnp.dot(xall[b, at], wbuf[s, b], preferred_element_type=F32)
        total = total.astype(BF16)
        for a in range(3):
            for h in range(3):
                start = a * 384 + h * 128
                tqkv[s, a, h, at, 0:128] = total[:, start : start + 128]

    def time_heads(s):
        for h in range(3):
            q, k = tqkv[s, 0, h, :, 0:128], tqkv[s, 1, h, :, 0:128]
            scores = lax.dot_general(q, k, (((1,), (1,)), ((), ())), preferred_element_type=F32)
            scores = jnp.where(same, scores.reshape(32, 16, 512), -jnp.inf).reshape(512, 512)
            obuf[s, :, h * 128 : (h + 1) * 128] = softmax_parts(scores, tqkv[s, 2, h]).astype(BF16)

    group_rows = pl.ds(pl.multiple_of((y * 16 + z * 2 + c) * 16, 16), 16)

    for d in range(2):
        bytes_wait(xall.at[0, 0:128], p3_recv.at[2, d])
    project(0, 0)
    forward(3)
    part_wait(w2_recv.at[1])
    to_core(1 - odd, 1)
    lax.fori_loop(4, 8, send_mixed, 0)
    bytes_wait(wbuf.at[1, :, 0:384], w3_recv.at[0])
    project(1, 0)
    for d in range(2, 4):
        bytes_wait(xall.at[0, 0:128], p3_recv.at[2, d])

    def half(s, _):
        project(s, 1)
        time_heads(s)
        zl_to = (zl + s) % 2

        def to(i, _):
            f_to = (f + i) % 32
            remote(
                obuf.at[s, pl.ds(pl.multiple_of((y + 4 - f_to // 8) % 4 * 128 + (f_to % 8) * 16, 16), 16)],
                time_out.at[group_rows],
                p5_send.at[0],
                p5_recv.at[0],
                (f_to, zl_to * 4 + x),
            ).start()
            return 0

        return lax.fori_loop(jnp.where(s == 0, 1, 0), 32, to, 0)

    lax.fori_loop(0, 2, half, 0)
    mine_out = pltpu.make_async_copy(
        obuf.at[0, pl.ds(pl.multiple_of((f % 8) * 16, 16), 16)], time_out.at[group_rows], own_sem.at[3]
    )
    mine_out.start()

    mine_mixed.wait()
    mine_out.wait()
    bytes_wait(hbuf.at[0:7], mb_recv.at[0])
    bytes_wait(mbuf.at[0:1008], p5_recv.at[0])
    for a in range(3):
        bytes_wait(kbuf.at[:, 0:7], p1_send.at[a])
    bytes_wait(hbuf.at[0:7], h_send.at[0])
    bytes_wait(wbuf.at[1, 0:2, 0:384], w_send.at[0])
    bytes_wait(wbuf.at[1, 0:2, 0:384], w_send.at[1])
    bytes_wait(wbuf.at[1, :, 0:384], w_send.at[2])
    bytes_wait(mbuf.at[0:1008], p2_send.at[0])
    bytes_wait(xall.at[0:2], p3_send.at[0])
    bytes_wait(xall.at[0], p3_send.at[1])
    bytes_wait(hbuf.at[0:7], mb_send.at[0])
    bytes_wait(mbuf.at[0:1008], p5_send.at[0])


def copy_kernel(mixed, out, mixed_to, out_to, mixed_held, out_held, sem):
    steps = []
    for i in range(4):
        for n, (src, held, dst, rows) in enumerate(
            ((mixed, mixed_held, mixed_to, pl.ds(i * 32, 32)), (out, out_held, out_to, pl.ds(i * 256, 256)))
        ):
            steps.append(
                (
                    pltpu.make_async_copy(src.at[rows], held.at[rows], sem.at[0, n, i]),
                    pltpu.make_async_copy(held.at[rows], dst.at[rows], sem.at[1, n, i]),
                )
            )
    for read, _ in steps:
        read.start()
    for read, write in steps:
        read.wait()
        write.start()
    for _, write in steps:
        write.wait()


def copy_out(mixed, out):
    anywhere = pl.BlockSpec(memory_space=pl.ANY)
    return pl.pallas_call(
        copy_kernel,
        out_shape=(jax.ShapeDtypeStruct(mixed.shape, mixed.dtype), jax.ShapeDtypeStruct(out.shape, out.dtype)),
        in_specs=[anywhere] * 2,
        out_specs=(anywhere, anywhere),
        scratch_shapes=[
            pltpu.VMEM(mixed.shape, mixed.dtype),
            pltpu.VMEM(out.shape, out.dtype),
            pltpu.SemaphoreType.DMA((2, 2, 4)),
        ],
        compiler_params=pltpu.CompilerParams(vmem_limit_bytes=58 << 20),
    )(mixed, out)


def on_device(hidden, queries, view_keys, view_values, ref_keys, ref_values, temporal_query, temporal_key, temporal_value):
    flat = [a.reshape(128, 3072) for a in (hidden, queries, view_keys, view_values, ref_keys, ref_values)]
    dma = pltpu.SemaphoreType.DMA
    mixed, out = pl.pallas_call(
        kernel,
        out_shape=(jax.ShapeDtypeStruct((128, 3072), BF16), jax.ShapeDtypeStruct((1024, 384), BF16)),
        in_specs=[pl.BlockSpec(memory_space=pl.ANY)] * 9,
        out_specs=(pl.BlockSpec(memory_space=pl.ANY), pl.BlockSpec(memory_space=pl.ANY)),
        scratch_shapes=[
            pltpu.VMEM((3, 8, 128, 128), BF16),
            pltpu.VMEM((3, 9, 128, 128), BF16),
            pltpu.VMEM((3, 9, 128, 256), BF16),
            pltpu.VMEM((8, 128, 384), BF16),
            pltpu.VMEM((3, 8, 128, 128), F32),
            pltpu.VMEM((1024, 384), BF16),
            pltpu.VMEM((4, 512, 768), BF16),
            pltpu.VMEM((2, 4, 768, 1152), BF16),
            pltpu.VMEM((2, 3, 3, 512, 256), BF16),
            pltpu.VMEM((2, 512, 384), BF16),
            dma((3,)), dma((3, 3)), dma((3, 3)), dma((1,)), dma((1,)), dma((1,)), dma((3,)), dma((2,)), dma((2,)), dma((1,)),
            dma((1,)), dma((4,)), dma((2,)), dma((3, 4)), dma((1,)), dma((1,)), dma((1,)), dma((1,)), dma((4,)),
            pltpu.SemaphoreType.REGULAR((1,)), pltpu.SemaphoreType.REGULAR((1,)),
        ],
        compiler_params=pltpu.CompilerParams(
            collective_id=0, has_side_effects=True, vmem_limit_bytes=58 << 20
        ),
    )(*flat, temporal_query, temporal_key, temporal_value)
    mixed, out = copy_out(mixed, out)
    return mixed.reshape(1, 1, 128, 3072), out.reshape(1, 8, 128, 384)


def solution(mesh):
    placed = (
        P("frame", "view", None, None),
        P("frame", "view", None, None),
        P("frame", "view", None, None),
        P("frame", "view", None, None),
        P("frame", None, None),
        P("frame", None, None),
        P(None, "view"),
        P(None, "view"),
        P(None, "view"),
    )
    return jax.shard_map(
        on_device,
        mesh=mesh,
        in_specs=placed,
        out_specs=(P("frame", "view", None, None), P("frame", None, None, "view")),
        check_vma=False,
    )
```

```python
import functools

import jax
import jax.numpy as jnp
from jax import lax
from jax.experimental import pallas as pl
from jax.experimental.pallas import tpu as pltpu
from jax.sharding import PartitionSpec as P

MESH = pl.DeviceIdType.MESH
BF16 = jnp.bfloat16
F32 = jnp.float32
SCALE = 128 ** (-0.5) * 1.4426950408889634


def softmax_parts(scores, values):
    top = jnp.max(scores, axis=-1, keepdims=True)
    weights = jnp.exp2((scores - top) * SCALE).astype(BF16)
    product = jnp.dot(weights, values, preferred_element_type=F32)
    return product[:, :128] / product[:, 128:]


def bytes_wait(ref, sem):
    pltpu.make_async_copy(ref, ref, sem).wait()


def kernel(
    hid, qry, key, val, rkey, rval, wq, wk, wv,
    mixed_out, time_out,
    qbuf, kbuf, vbuf, hbuf, abuf, mbuf, xall, wbuf, tqkv, obuf,
    p1_send, p1_recv, loc, h_send, h_recv, wl_sem, w_send, w1_recv, w2_recv, w3_recv, w4_recv,
    p2_send, p2_recv, p3_send, p3_recv, mb_send, mb_recv, p5_send, p5_recv, own_sem,
    core_in, plane_in,
):
    f = lax.axis_index("frame")
    v = lax.axis_index("view")
    y, zh, c = f // 8, (f // 2) % 4, f % 2
    zl, x = v // 4, v % 4
    z = zh * 2 + zl
    z_skip = 1 + 6 * zl

    def device(y_, z_, c_, x_):
        return (y_ * 8 + (z_ // 2) * 2 + c_, (z_ % 2) * 4 + x_)

    def column(part, width=384):
        return pl.ds(pl.multiple_of(part * width, width), width)

    def remote(src, dst, send, recv, target):
        return pltpu.make_async_remote_copy(
            src_ref=src, dst_ref=dst, send_sem=send, recv_sem=recv, device_id=target, device_id_type=MESH
        )

    barrier = pltpu.get_barrier_semaphore()

    def greet(target, sem=barrier):
        pl.semaphore_signal(sem, inc=1, device_id=target, device_id_type=MESH)

    def greet_view(i, _):
        greet((f, (v + i) % 8))
        return 0

    def greet_z(i, _):
        greet(device(y, (z + i) % 8, c, x))
        return 0

    def greet_y(i, _):
        greet(device((y + i) % 4, z, c, x))
        return 0

    lax.fori_loop(1, 8, greet_view, 0)
    lax.fori_loop(1, 7, lambda i, _: greet_z(i + jnp.where(i >= z_skip, 1, 0), _), 0)
    lax.fori_loop(1, 4, greet_y, 0)
    greet(device(y, z, 1 - c, x))

    def local_heads(h, _):
        cols = pl.ds(pl.multiple_of(v * 384 + h * 128, 128), 128)
        pltpu.make_async_copy(qry.at[:, cols], qbuf.at[h, v], loc.at[h, 0]).start()
        pltpu.make_async_copy(key.at[:, cols], kbuf.at[h, v], loc.at[h, 1]).start()
        pltpu.make_async_copy(rkey.at[:, cols], kbuf.at[h, 8], loc.at[h, 1]).start()
        pltpu.make_async_copy(val.at[:, cols], vbuf.at[h, v, :, 0:128], loc.at[h, 2]).start()
        pltpu.make_async_copy(rval.at[:, cols], vbuf.at[h, 8, :, 0:128], loc.at[h, 2]).start()
        return 0

    lax.fori_loop(0, 3, local_heads, 0)
    pltpu.make_async_copy(hid.at[:, column(v)], hbuf.at[v], own_sem.at[0]).start()

    def load_weights(i, _):
        rows = column(i)
        place = pl.ds(pl.multiple_of((i // 4) * 384, 384), 384)
        for a, w in enumerate((wq, wk, wv)):
            pltpu.make_async_copy(
                w.at[rows], wbuf.at[0, i % 4, place, a * 384 : (a + 1) * 384], wl_sem.at[0]
            ).start()
        return 0

    pl.semaphore_wait(barrier, 17)

    z_far = (z + 7 + 2 * zl) % 8
    part_at = pl.ds(pl.multiple_of(c * 384, 384), 384)

    def piece(y_, a):
        return wbuf.at[1, y_, part_at, a * 384 : (a + 1) * 384]

    def bring(a):
        source = (wq, wk, wv)[a].at[column(c * 4 + y)]
        remote(source, piece(y, a), w_send.at[0], w1_recv.at[a], device(y, z_far, c, x)).start()

    def to_core(y_, a):
        place = piece(y_, a)
        remote(place, place, w_send.at[2], w3_recv.at[0], device(y, z, 1 - c, x)).start()

    def pass_on(a):
        place = piece(y, a)
        bytes_wait(place, w1_recv.at[a])
        for n in range(2):
            remote(place, place, w_send.at[1], w2_recv.at[n, a], device((y + 1 + 2 * n) % 4, z, c, x)).start()
        to_core(y, a)

    def pass_far(a):
        for n in range(2):
            from_y = (y + 3 + 2 * n) % 4
            bytes_wait(piece(y, a), w2_recv.at[n, a])
            rows = pl.ds(pl.multiple_of(c * 384 + n * 192, 192), 192)
            place = wbuf.at[1, from_y, rows, a * 384 : (a + 1) * 384]
            remote(place, place, w_send.at[1], w4_recv.at[a], device((y + 1 + 2 * n) % 4, z, c, x)).start()
            to_core(from_y, a)

    def pass_last(a):
        bytes_wait(piece(y, a), w4_recv.at[a])
        to_core((y + 2) % 4, a)

    for a in range(3):
        bring(a)

    def send_heads(h, _):
        def to(i, _):
            w = (v + i) % 8
            cols = pl.ds(pl.multiple_of(w * 384 + h * 128, 128), 128)
            remote(key.at[:, cols], kbuf.at[h, v], p1_send.at[1], p1_recv.at[h, 1], (f, w)).start()
            remote(qry.at[:, cols], qbuf.at[h, v], p1_send.at[0], p1_recv.at[h, 0], (f, w)).start()
            remote(val.at[:, cols], vbuf.at[h, v, :, 0:128], p1_send.at[2], p1_recv.at[h, 2], (f, w)).start()
            return 0

        return lax.fori_loop(1, 8, to, 0)

    lax.fori_loop(0, 3, send_heads, 0)

    def send_hidden(i, _):
        w = (v + i) % 8
        remote(hid.at[:, column(w)], hbuf.at[v], h_send.at[0], h_recv.at[0], (f, w)).start()
        return 0

    lax.fori_loop(1, 8, send_hidden, 0)

    greet(device(y, z, 1 - c, x), core_in.at[0])
    lax.fori_loop(0, 8, load_weights, 0)

    vbuf[:, :, :, 128:256] = jnp.ones((3, 9, 128, 128), BF16)
    tqkv[:, 2, :, :, 128:256] = jnp.ones((2, 3, 512, 128), BF16)

    def view_head(h, _):
        bytes_wait(kbuf.at[h, 0:2], loc.at[h, 1])
        bytes_wait(qbuf.at[h, 0:1], loc.at[h, 0])
        bytes_wait(kbuf.at[h, 0:2], loc.at[h, 2])
        bytes_wait(qbuf.at[h, 0:7], p1_recv.at[h, 0])
        bytes_wait(kbuf.at[h, 0:7], p1_recv.at[h, 1])
        bytes_wait(kbuf.at[h, 0:7], p1_recv.at[h, 2])
        keys = kbuf[h].reshape(1152, 128)
        values = vbuf[h].reshape(1152, 256)

        def rows(r, _):
            q = qbuf[h, pl.ds(r * 2, 2)].reshape(256, 128)
            scores = lax.dot_general(q, keys, (((1,), (1,)), ((), ())), preferred_element_type=F32)
            abuf[h, pl.ds(r * 2, 2)] = softmax_parts(scores, values).reshape(2, 128, 128)
            return 0

        return lax.fori_loop(0, 4, rows, 0)

    pl.semaphore_wait(core_in.at[0], 1)
    for i in range(1, 4):
        greet(device((y + i) % 4, z, c, x), plane_in.at[0])
    pass_on(0)
    lax.fori_loop(0, 1, view_head, 0)
    pass_on(1)
    lax.fori_loop(1, 2, view_head, 0)
    pass_on(2)
    pass_far(0)
    lax.fori_loop(2, 3, view_head, 0)
    pass_far(1)
    pass_far(2)
    pl.semaphore_wait(plane_in.at[0], 3)

    bytes_wait(hbuf.at[0:1], own_sem.at[0])
    bytes_wait(hbuf.at[0:7], h_recv.at[0])

    def residual(i, _):
        views = pl.ds(i * 2, 2)
        block = hbuf[views].astype(F32) + jnp.concatenate([abuf[h, views] for h in range(3)], axis=-1)
        mbuf[pl.ds(pl.multiple_of(i * 256, 256), 256)] = block.reshape(256, 384).astype(BF16)
        return 0

    lax.fori_loop(0, 4, residual, 0)

    def tokens_out(n, _):
        d = n
        y_to = (y + d) % 4

        def to(j, _):
            z_to, c_to = (z + j // 2) % 8, (c + j % 2) % 2
            group = y_to * 16 + z_to * 2 + c_to
            source = mbuf.at[pl.ds(pl.multiple_of(group * 16, 16), 16)]
            place = xall.at[x, pl.ds(pl.multiple_of(d * 128 + (f % 8) * 16, 16), 16), column(zl)]
            here = (d == 0) & (j == 0)

            @pl.when(here)
            def _():
                pltpu.make_async_copy(source, place, p2_recv.at[0]).start()

            @pl.when(jnp.logical_not(here))
            def _():
                remote(source, place, p2_send.at[0], p2_recv.at[d], device(y_to, z_to, c_to, x)).start()

            return 0

        return lax.fori_loop(0, 16, to, 0)

    def send_mixed(i, _):
        w = (zl + i // 4) % 2 * 4 + (x + i % 4) % 4
        remote(
            mbuf.at[pl.ds(pl.multiple_of(w * 128, 128), 128)],
            mixed_out.at[:, column(v)],
            mb_send.at[0],
            mb_recv.at[0],
            (f, w),
        ).start()
        return 0

    def x_device(i):
        return (f, zl * 4 + (x + i) % 4)

    def direct(d):
        rows = pl.ds(pl.multiple_of(d * 128, 128), 128)
        remote(xall.at[x, rows], xall.at[x, rows], p3_send.at[0], p3_recv.at[0, d], x_device(1)).start()
        remote(xall.at[x, rows], xall.at[x, rows], p3_send.at[0], p3_recv.at[1, d], x_device(3)).start()

    def forward(d):
        for n in range(2):
            bytes_wait(xall.at[0, 0:128], p3_recv.at[n, d])
            rows = pl.ds(pl.multiple_of(d * 128 + n * 64, 64), 64)
            block = xall.at[(x + 3 + 2 * n) % 4, rows]
            remote(block, block, p3_send.at[1], p3_recv.at[2, d], x_device(1 + 2 * n)).start()

    def step(t, _):
        @pl.when(t < 4)
        def _():
            tokens_out(t, 0)

        @pl.when(t == 0)
        def _():
            lax.fori_loop(1, 4, send_mixed, 0)

        @pl.when(t >= 1)
        def _():
            bytes_wait(mbuf.at[0:256], p2_recv.at[t - 1])
            direct(t - 1)

        @pl.when(t >= 2)
        def _():
            forward(t - 2)

        return 0

    lax.fori_loop(0, 5, step, 0)
    mine_mixed = pltpu.make_async_copy(
        mbuf.at[pl.ds(pl.multiple_of(v * 128, 128), 128)], mixed_out.at[:, column(v)], own_sem.at[2]
    )
    mine_mixed.start()

    bytes_wait(wbuf.at[0], wl_sem.at[0])

    row = lax.broadcasted_iota(jnp.int32, (1, 16, 512), 1)
    col = lax.broadcasted_iota(jnp.int32, (1, 16, 512), 2)
    same = row == col % 16

    def project(s, r):
        at = pl.ds(pl.multiple_of(r * 256, 256), 256)
        total = jnp.dot(xall[0, at], wbuf[s, 0], preferred_element_type=F32)
        for b in range(1, 4):
            total += jnp.dot(xall[b, at], wbuf[s, b], preferred_element_type=F32)
        total = total.astype(BF16)
        for a in range(3):
            for h in range(3):
                start = a * 384 + h * 128
                tqkv[s, a, h, at, 0:128] = total[:, start : start + 128]

    def time_heads(s):
        for h in range(3):
            q, k = tqkv[s, 0, h, :, 0:128], tqkv[s, 1, h, :, 0:128]
            scores = lax.dot_general(q, k, (((1,), (1,)), ((), ())), preferred_element_type=F32)
            scores = jnp.where(same, scores.reshape(32, 16, 512), -jnp.inf).reshape(512, 512)
            obuf[s, :, h * 128 : (h + 1) * 128] = softmax_parts(scores, tqkv[s, 2, h]).astype(BF16)

    group_rows = pl.ds(pl.multiple_of((y * 16 + z * 2 + c) * 16, 16), 16)

    for d in range(2):
        bytes_wait(xall.at[0, 0:128], p3_recv.at[2, d])
    project(0, 0)
    forward(3)
    for a in range(3):
        pass_last(a)
    bytes_wait(wbuf.at[1, :, 0:384], w3_recv.at[0])
    lax.fori_loop(4, 8, send_mixed, 0)
    project(1, 0)
    for d in range(2, 4):
        bytes_wait(xall.at[0, 0:128], p3_recv.at[2, d])

    def half(s, _):
        project(s, 1)
        time_heads(s)
        zl_to = (zl + s) % 2

        def to(i, _):
            f_to = (f + i) % 32
            remote(
                obuf.at[s, pl.ds(pl.multiple_of((y + 4 - f_to // 8) % 4 * 128 + (f_to % 8) * 16, 16), 16)],
                time_out.at[group_rows],
                p5_send.at[0],
                p5_recv.at[0],
                (f_to, zl_to * 4 + x),
            ).start()
            return 0

        return lax.fori_loop(jnp.where(s == 0, 1, 0), 32, to, 0)

    lax.fori_loop(0, 2, half, 0)
    mine_out = pltpu.make_async_copy(
        obuf.at[0, pl.ds(pl.multiple_of((f % 8) * 16, 16), 16)], time_out.at[group_rows], own_sem.at[3]
    )
    mine_out.start()

    mine_mixed.wait()
    mine_out.wait()
    bytes_wait(hbuf.at[0:7], mb_recv.at[0])
    bytes_wait(mbuf.at[0:1008], p5_recv.at[0])
    for a in range(3):
        bytes_wait(kbuf.at[:, 0:7], p1_send.at[a])
    bytes_wait(hbuf.at[0:7], h_send.at[0])
    bytes_wait(wbuf.at[1, 0, 0:384], w_send.at[0])
    bytes_wait(wbuf.at[1, 0:3, 0:384], w_send.at[1])
    bytes_wait(wbuf.at[1, :, 0:384], w_send.at[2])
    bytes_wait(mbuf.at[0:1008], p2_send.at[0])
    bytes_wait(xall.at[0:2], p3_send.at[0])
    bytes_wait(xall.at[0], p3_send.at[1])
    bytes_wait(hbuf.at[0:7], mb_send.at[0])
    bytes_wait(mbuf.at[0:1008], p5_send.at[0])


def copy_kernel(mixed, out, mixed_to, out_to, mixed_held, out_held, sem):
    steps = []
    for i in range(4):
        for n, (src, held, dst, rows) in enumerate(
            ((mixed, mixed_held, mixed_to, pl.ds(i * 32, 32)), (out, out_held, out_to, pl.ds(i * 256, 256)))
        ):
            steps.append(
                (
                    pltpu.make_async_copy(src.at[rows], held.at[rows], sem.at[0, n, i]),
                    pltpu.make_async_copy(held.at[rows], dst.at[rows], sem.at[1, n, i]),
                )
            )
    for read, _ in steps:
        read.start()
    for read, write in steps:
        read.wait()
        write.start()
    for _, write in steps:
        write.wait()


def copy_out(mixed, out):
    anywhere = pl.BlockSpec(memory_space=pl.ANY)
    return pl.pallas_call(
        copy_kernel,
        out_shape=(jax.ShapeDtypeStruct(mixed.shape, mixed.dtype), jax.ShapeDtypeStruct(out.shape, out.dtype)),
        in_specs=[anywhere] * 2,
        out_specs=(anywhere, anywhere),
        scratch_shapes=[
            pltpu.VMEM(mixed.shape, mixed.dtype),
            pltpu.VMEM(out.shape, out.dtype),
            pltpu.SemaphoreType.DMA((2, 2, 4)),
        ],
        compiler_params=pltpu.CompilerParams(vmem_limit_bytes=58 << 20),
    )(mixed, out)


def on_device(hidden, queries, view_keys, view_values, ref_keys, ref_values, temporal_query, temporal_key, temporal_value):
    flat = [a.reshape(128, 3072) for a in (hidden, queries, view_keys, view_values, ref_keys, ref_values)]
    dma = pltpu.SemaphoreType.DMA
    mixed, out = pl.pallas_call(
        kernel,
        out_shape=(jax.ShapeDtypeStruct((128, 3072), BF16), jax.ShapeDtypeStruct((1024, 384), BF16)),
        in_specs=[pl.BlockSpec(memory_space=pl.ANY)] * 9,
        out_specs=(pl.BlockSpec(memory_space=pl.ANY), pl.BlockSpec(memory_space=pl.ANY)),
        scratch_shapes=[
            pltpu.VMEM((3, 8, 128, 128), BF16),
            pltpu.VMEM((3, 9, 128, 128), BF16),
            pltpu.VMEM((3, 9, 128, 256), BF16),
            pltpu.VMEM((8, 128, 384), BF16),
            pltpu.VMEM((3, 8, 128, 128), F32),
            pltpu.VMEM((1024, 384), BF16),
            pltpu.VMEM((4, 512, 768), BF16),
            pltpu.VMEM((2, 4, 768, 1152), BF16),
            pltpu.VMEM((2, 3, 3, 512, 256), BF16),
            pltpu.VMEM((2, 512, 384), BF16),
            dma((3,)), dma((3, 3)), dma((3, 3)), dma((1,)), dma((1,)), dma((1,)), dma((3,)), dma((3,)), dma((2, 3)), dma((1,)), dma((3,)),
            dma((2,)), dma((4,)), dma((2,)), dma((3, 4)), dma((1,)), dma((1,)), dma((1,)), dma((1,)), dma((4,)),
            pltpu.SemaphoreType.REGULAR((1,)), pltpu.SemaphoreType.REGULAR((1,)),
        ],
        compiler_params=pltpu.CompilerParams(
            collective_id=0, has_side_effects=True, vmem_limit_bytes=58 << 20
        ),
    )(*flat, temporal_query, temporal_key, temporal_value)
    mixed, out = copy_out(mixed, out)
    return mixed.reshape(1, 1, 128, 3072), out.reshape(1, 8, 128, 384)


def solution(mesh):
    placed = (
        P("frame", "view", None, None),
        P("frame", "view", None, None),
        P("frame", "view", None, None),
        P("frame", "view", None, None),
        P("frame", None, None),
        P("frame", None, None),
        P(None, "view"),
        P(None, "view"),
        P(None, "view"),
    )
    return jax.shard_map(
        on_device,
        mesh=mesh,
        in_specs=placed,
        out_specs=(P("frame", "view", None, None), P("frame", None, None, "view")),
        check_vma=False,
    )
```

```python
import functools

import jax
import jax.numpy as jnp
from jax import lax
from jax.experimental import pallas as pl
from jax.experimental.pallas import tpu as pltpu
from jax.sharding import PartitionSpec as P

MESH = pl.DeviceIdType.MESH
BF16 = jnp.bfloat16
F32 = jnp.float32
SCALE = 128 ** (-0.5) * 1.4426950408889634


def softmax_parts(scores, values):
    top = jnp.max(scores, axis=-1, keepdims=True)
    weights = jnp.exp2((scores - top) * SCALE).astype(BF16)
    product = jnp.dot(weights, values, preferred_element_type=F32)
    return product[:, :128] / product[:, 128:]


def bytes_wait(ref, sem):
    pltpu.make_async_copy(ref, ref, sem).wait()


def kernel(
    hid, qry, key, val, rkey, rval, wq, wk, wv,
    mixed_out, time_out,
    qbuf, kbuf, vbuf, hbuf, abuf, mbuf, xall, wbuf, tqkv, obuf,
    p1_send, p1_recv, loc, h_send, h_recv, wl_sem, w_send, w1_recv, w2_recv, w3_recv, w4_recv,
    p2_send, p2_recv, p3_send, p3_recv, mb_send, mb_recv, p5_send, p5_recv, own_sem,
    core_in, plane_in,
):
    f = lax.axis_index("frame")
    v = lax.axis_index("view")
    y, zh, c = f // 8, (f // 2) % 4, f % 2
    zl, x = v // 4, v % 4
    z = zh * 2 + zl
    z_skip = 1 + 6 * zl

    def device(y_, z_, c_, x_):
        return (y_ * 8 + (z_ // 2) * 2 + c_, (z_ % 2) * 4 + x_)

    def column(part, width=384):
        return pl.ds(pl.multiple_of(part * width, width), width)

    def remote(src, dst, send, recv, target):
        return pltpu.make_async_remote_copy(
            src_ref=src, dst_ref=dst, send_sem=send, recv_sem=recv, device_id=target, device_id_type=MESH
        )

    barrier = pltpu.get_barrier_semaphore()

    def greet(target, sem=barrier):
        pl.semaphore_signal(sem, inc=1, device_id=target, device_id_type=MESH)

    def greet_view(i, _):
        greet((f, (v + i) % 8))
        return 0

    def greet_z(i, _):
        greet(device(y, (z + i) % 8, c, x))
        return 0

    def greet_y(i, _):
        greet(device((y + i) % 4, z, c, x))
        return 0

    lax.fori_loop(1, 8, greet_view, 0)
    lax.fori_loop(1, 7, lambda i, _: greet_z(i + jnp.where(i >= z_skip, 1, 0), _), 0)
    lax.fori_loop(1, 4, greet_y, 0)
    greet(device(y, z, 1 - c, x))

    def local_heads(h, _):
        cols = pl.ds(pl.multiple_of(v * 384 + h * 128, 128), 128)
        pltpu.make_async_copy(qry.at[:, cols], qbuf.at[h, v], loc.at[h, 0]).start()
        pltpu.make_async_copy(key.at[:, cols], kbuf.at[h, v], loc.at[h, 1]).start()
        pltpu.make_async_copy(rkey.at[:, cols], kbuf.at[h, 8], loc.at[h, 1]).start()
        pltpu.make_async_copy(val.at[:, cols], vbuf.at[h, v, :, 0:128], loc.at[h, 2]).start()
        pltpu.make_async_copy(rval.at[:, cols], vbuf.at[h, 8, :, 0:128], loc.at[h, 2]).start()
        return 0

    lax.fori_loop(0, 3, local_heads, 0)
    pltpu.make_async_copy(hid.at[:, column(v)], hbuf.at[v], own_sem.at[0]).start()

    def load_weights(i, _):
        rows = column(i)
        place = pl.ds(pl.multiple_of((i // 4) * 384, 384), 384)
        for a, w in enumerate((wq, wk, wv)):
            pltpu.make_async_copy(
                w.at[rows], wbuf.at[0, i % 4, place, a * 384 : (a + 1) * 384], wl_sem.at[0]
            ).start()
        return 0

    pl.semaphore_wait(barrier, 17)

    z_far = (z + 7 + 2 * zl) % 8
    part_at = pl.ds(pl.multiple_of(c * 384, 384), 384)

    def piece(y_, a):
        return wbuf.at[1, y_, part_at, a * 384 : (a + 1) * 384]

    def bring(a):
        source = (wq, wk, wv)[a].at[column(c * 4 + y)]
        remote(source, piece(y, a), w_send.at[0], w1_recv.at[a], device(y, z_far, c, x)).start()

    def to_core(y_, a):
        place = piece(y_, a)
        remote(place, place, w_send.at[2], w3_recv.at[0], device(y, z, 1 - c, x)).start()

    def pass_on(a):
        place = piece(y, a)
        bytes_wait(place, w1_recv.at[a])
        for n in range(2):
            remote(place, place, w_send.at[1], w2_recv.at[n, a], device((y + 1 + 2 * n) % 4, z, c, x)).start()
        to_core(y, a)

    def pass_far(a):
        for n in range(2):
            from_y = (y + 3 + 2 * n) % 4
            bytes_wait(piece(y, a), w2_recv.at[n, a])
            rows = pl.ds(pl.multiple_of(c * 384 + n * 192, 192), 192)
            place = wbuf.at[1, from_y, rows, a * 384 : (a + 1) * 384]
            remote(place, place, w_send.at[1], w4_recv.at[a], device((y + 1 + 2 * n) % 4, z, c, x)).start()
            to_core(from_y, a)

    def pass_last(a):
        bytes_wait(piece(y, a), w4_recv.at[a])
        to_core((y + 2) % 4, a)

    for a in range(3):
        bring(a)

    def send_heads(h, _):
        def to(i, _):
            w = (v + i) % 8
            cols = pl.ds(pl.multiple_of(w * 384 + h * 128, 128), 128)
            remote(key.at[:, cols], kbuf.at[h, v], p1_send.at[1], p1_recv.at[h, 1], (f, w)).start()
            remote(qry.at[:, cols], qbuf.at[h, v], p1_send.at[0], p1_recv.at[h, 0], (f, w)).start()
            remote(val.at[:, cols], vbuf.at[h, v, :, 0:128], p1_send.at[2], p1_recv.at[h, 2], (f, w)).start()
            return 0

        return lax.fori_loop(1, 8, to, 0)

    lax.fori_loop(0, 3, send_heads, 0)

    def send_hidden(i, _):
        w = (v + i) % 8
        remote(hid.at[:, column(w)], hbuf.at[v], h_send.at[0], h_recv.at[0], (f, w)).start()
        return 0

    lax.fori_loop(1, 8, send_hidden, 0)

    greet(device(y, z, 1 - c, x), core_in.at[0])
    lax.fori_loop(0, 8, load_weights, 0)

    vbuf[:, :, :, 128:256] = jnp.ones((3, 9, 128, 128), BF16)
    tqkv[:, 2, :, :, 128:256] = jnp.ones((2, 3, 512, 128), BF16)

    def view_head(h, _):
        bytes_wait(kbuf.at[h, 0:2], loc.at[h, 1])
        bytes_wait(qbuf.at[h, 0:1], loc.at[h, 0])
        bytes_wait(kbuf.at[h, 0:2], loc.at[h, 2])
        bytes_wait(qbuf.at[h, 0:7], p1_recv.at[h, 0])
        bytes_wait(kbuf.at[h, 0:7], p1_recv.at[h, 1])
        bytes_wait(kbuf.at[h, 0:7], p1_recv.at[h, 2])
        keys = kbuf[h].reshape(1152, 128)
        values = vbuf[h].reshape(1152, 256)

        def rows(r, _):
            q = qbuf[h, pl.ds(r * 2, 2)].reshape(256, 128)
            scores = lax.dot_general(q, keys, (((1,), (1,)), ((), ())), preferred_element_type=F32)
            abuf[h, pl.ds(r * 2, 2)] = softmax_parts(scores, values).reshape(2, 128, 128)
            return 0

        return lax.fori_loop(0, 4, rows, 0)

    pl.semaphore_wait(core_in.at[0], 1)
    for i in range(1, 4):
        greet(device((y + i) % 4, z, c, x), plane_in.at[0])
    pass_on(0)
    lax.fori_loop(0, 1, view_head, 0)
    pass_on(1)
    lax.fori_loop(1, 2, view_head, 0)
    pass_on(2)
    pass_far(0)
    lax.fori_loop(2, 3, view_head, 0)
    pass_far(1)
    pass_far(2)
    pl.semaphore_wait(plane_in.at[0], 3)

    bytes_wait(hbuf.at[0:1], own_sem.at[0])
    bytes_wait(hbuf.at[0:7], h_recv.at[0])

    def residual(i, _):
        views = pl.ds(i * 2, 2)
        block = hbuf[views].astype(F32) + jnp.concatenate([abuf[h, views] for h in range(3)], axis=-1)
        mbuf[pl.ds(pl.multiple_of(i * 256, 256), 256)] = block.reshape(256, 384).astype(BF16)
        return 0

    lax.fori_loop(0, 4, residual, 0)

    def tokens_out(n, _):
        d = n
        y_to = (y + d) % 4

        def to(j, _):
            m = j // 2
            z_to = (z + jnp.where(m % 2 == 1, (m + 1) // 2, 8 - m // 2)) % 8
            c_to = (c + j % 2) % 2
            group = y_to * 16 + z_to * 2 + c_to
            source = mbuf.at[pl.ds(pl.multiple_of(group * 16, 16), 16)]
            place = xall.at[x, pl.ds(pl.multiple_of(d * 128 + (f % 8) * 16, 16), 16), column(zl)]
            here = (d == 0) & (j == 0)

            @pl.when(here)
            def _():
                pltpu.make_async_copy(source, place, p2_recv.at[0]).start()

            @pl.when(jnp.logical_not(here))
            def _():
                remote(source, place, p2_send.at[0], p2_recv.at[d], device(y_to, z_to, c_to, x)).start()

            return 0

        return lax.fori_loop(0, 16, to, 0)

    def send_mixed(i, _):
        w = (zl + i // 4) % 2 * 4 + (x + i % 4) % 4
        remote(
            mbuf.at[pl.ds(pl.multiple_of(w * 128, 128), 128)],
            mixed_out.at[:, column(v)],
            mb_send.at[0],
            mb_recv.at[0],
            (f, w),
        ).start()
        return 0

    def x_device(i):
        return (f, zl * 4 + (x + i) % 4)

    def direct(d):
        rows = pl.ds(pl.multiple_of(d * 128, 128), 128)
        remote(xall.at[x, rows], xall.at[x, rows], p3_send.at[0], p3_recv.at[0, d], x_device(1)).start()
        remote(xall.at[x, rows], xall.at[x, rows], p3_send.at[0], p3_recv.at[1, d], x_device(3)).start()

    def forward(d):
        for n in range(2):
            bytes_wait(xall.at[0, 0:128], p3_recv.at[n, d])
            rows = pl.ds(pl.multiple_of(d * 128 + n * 64, 64), 64)
            block = xall.at[(x + 3 + 2 * n) % 4, rows]
            remote(block, block, p3_send.at[1], p3_recv.at[2, d], x_device(1 + 2 * n)).start()

    def step(t, _):
        @pl.when(t < 4)
        def _():
            tokens_out(t, 0)

        @pl.when(t == 0)
        def _():
            lax.fori_loop(1, 4, send_mixed, 0)

        @pl.when(t >= 1)
        def _():
            bytes_wait(mbuf.at[0:256], p2_recv.at[t - 1])
            direct(t - 1)

        @pl.when(t >= 2)
        def _():
            forward(t - 2)

        return 0

    lax.fori_loop(0, 5, step, 0)
    mine_mixed = pltpu.make_async_copy(
        mbuf.at[pl.ds(pl.multiple_of(v * 128, 128), 128)], mixed_out.at[:, column(v)], own_sem.at[2]
    )
    mine_mixed.start()

    bytes_wait(wbuf.at[0], wl_sem.at[0])

    row = lax.broadcasted_iota(jnp.int32, (1, 16, 512), 1)
    col = lax.broadcasted_iota(jnp.int32, (1, 16, 512), 2)
    same = row == col % 16

    def project(s, r):
        at = pl.ds(pl.multiple_of(r * 256, 256), 256)
        total = jnp.dot(xall[0, at], wbuf[s, 0], preferred_element_type=F32)
        for b in range(1, 4):
            total += jnp.dot(xall[b, at], wbuf[s, b], preferred_element_type=F32)
        total = total.astype(BF16)
        for a in range(3):
            for h in range(3):
                start = a * 384 + h * 128
                tqkv[s, a, h, at, 0:128] = total[:, start : start + 128]

    def time_heads(s):
        for h in range(3):
            q, k = tqkv[s, 0, h, :, 0:128], tqkv[s, 1, h, :, 0:128]
            scores = lax.dot_general(q, k, (((1,), (1,)), ((), ())), preferred_element_type=F32)
            scores = jnp.where(same, scores.reshape(32, 16, 512), -jnp.inf).reshape(512, 512)
            obuf[s, :, h * 128 : (h + 1) * 128] = softmax_parts(scores, tqkv[s, 2, h]).astype(BF16)

    group_rows = pl.ds(pl.multiple_of((y * 16 + z * 2 + c) * 16, 16), 16)

    for d in range(2):
        bytes_wait(xall.at[0, 0:128], p3_recv.at[2, d])
    project(0, 0)
    forward(3)
    for a in range(3):
        pass_last(a)
    bytes_wait(wbuf.at[1, :, 0:384], w3_recv.at[0])
    lax.fori_loop(4, 8, send_mixed, 0)
    project(1, 0)
    for d in range(2, 4):
        bytes_wait(xall.at[0, 0:128], p3_recv.at[2, d])

    def half(s, _):
        project(s, 1)
        time_heads(s)
        zl_to = (zl + s) % 2

        def to(i, _):
            n = (i // 2) % 4
            n = jnp.where(n >= 2, 5 - n, n)
            f_to = (y + i // 8) % 4 * 8 + (zh + n) % 4 * 2 + (c + i % 2) % 2
            remote(
                obuf.at[s, pl.ds(pl.multiple_of((y + 4 - f_to // 8) % 4 * 128 + (f_to % 8) * 16, 16), 16)],
                time_out.at[group_rows],
                p5_send.at[0],
                p5_recv.at[0],
                (f_to, zl_to * 4 + x),
            ).start()
            return 0

        return lax.fori_loop(jnp.where(s == 0, 1, 0), 32, to, 0)

    lax.fori_loop(0, 2, half, 0)
    mine_out = pltpu.make_async_copy(
        obuf.at[0, pl.ds(pl.multiple_of((f % 8) * 16, 16), 16)], time_out.at[group_rows], own_sem.at[3]
    )
    mine_out.start()

    mine_mixed.wait()
    mine_out.wait()
    bytes_wait(hbuf.at[0:7], mb_recv.at[0])
    bytes_wait(mbuf.at[0:1008], p5_recv.at[0])
    for a in range(3):
        bytes_wait(kbuf.at[:, 0:7], p1_send.at[a])
    bytes_wait(hbuf.at[0:7], h_send.at[0])
    bytes_wait(wbuf.at[1, 0, 0:384], w_send.at[0])
    bytes_wait(wbuf.at[1, 0:3, 0:384], w_send.at[1])
    bytes_wait(wbuf.at[1, :, 0:384], w_send.at[2])
    bytes_wait(mbuf.at[0:1008], p2_send.at[0])
    bytes_wait(xall.at[0:2], p3_send.at[0])
    bytes_wait(xall.at[0], p3_send.at[1])
    bytes_wait(hbuf.at[0:7], mb_send.at[0])
    bytes_wait(mbuf.at[0:1008], p5_send.at[0])


def copy_kernel(mixed, out, mixed_to, out_to, mixed_held, out_held, sem):
    steps = []
    for i in range(4):
        for n, (src, held, dst, rows) in enumerate(
            ((mixed, mixed_held, mixed_to, pl.ds(i * 32, 32)), (out, out_held, out_to, pl.ds(i * 256, 256)))
        ):
            steps.append(
                (
                    pltpu.make_async_copy(src.at[rows], held.at[rows], sem.at[0, n, i]),
                    pltpu.make_async_copy(held.at[rows], dst.at[rows], sem.at[1, n, i]),
                )
            )
    for read, _ in steps:
        read.start()
    for read, write in steps:
        read.wait()
        write.start()
    for _, write in steps:
        write.wait()


def copy_out(mixed, out):
    anywhere = pl.BlockSpec(memory_space=pl.ANY)
    return pl.pallas_call(
        copy_kernel,
        out_shape=(jax.ShapeDtypeStruct(mixed.shape, mixed.dtype), jax.ShapeDtypeStruct(out.shape, out.dtype)),
        in_specs=[anywhere] * 2,
        out_specs=(anywhere, anywhere),
        scratch_shapes=[
            pltpu.VMEM(mixed.shape, mixed.dtype),
            pltpu.VMEM(out.shape, out.dtype),
            pltpu.SemaphoreType.DMA((2, 2, 4)),
        ],
        compiler_params=pltpu.CompilerParams(vmem_limit_bytes=58 << 20),
    )(mixed, out)


def on_device(hidden, queries, view_keys, view_values, ref_keys, ref_values, temporal_query, temporal_key, temporal_value):
    flat = [a.reshape(128, 3072) for a in (hidden, queries, view_keys, view_values, ref_keys, ref_values)]
    dma = pltpu.SemaphoreType.DMA
    mixed, out = pl.pallas_call(
        kernel,
        out_shape=(jax.ShapeDtypeStruct((128, 3072), BF16), jax.ShapeDtypeStruct((1024, 384), BF16)),
        in_specs=[pl.BlockSpec(memory_space=pl.ANY)] * 9,
        out_specs=(pl.BlockSpec(memory_space=pl.ANY), pl.BlockSpec(memory_space=pl.ANY)),
        scratch_shapes=[
            pltpu.VMEM((3, 8, 128, 128), BF16),
            pltpu.VMEM((3, 9, 128, 128), BF16),
            pltpu.VMEM((3, 9, 128, 256), BF16),
            pltpu.VMEM((8, 128, 384), BF16),
            pltpu.VMEM((3, 8, 128, 128), F32),
            pltpu.VMEM((1024, 384), BF16),
            pltpu.VMEM((4, 512, 768), BF16),
            pltpu.VMEM((2, 4, 768, 1152), BF16),
            pltpu.VMEM((2, 3, 3, 512, 256), BF16),
            pltpu.VMEM((2, 512, 384), BF16),
            dma((3,)), dma((3, 3)), dma((3, 3)), dma((1,)), dma((1,)), dma((1,)), dma((3,)), dma((3,)), dma((2, 3)), dma((1,)), dma((3,)),
            dma((2,)), dma((4,)), dma((2,)), dma((3, 4)), dma((1,)), dma((1,)), dma((1,)), dma((1,)), dma((4,)),
            pltpu.SemaphoreType.REGULAR((1,)), pltpu.SemaphoreType.REGULAR((1,)),
        ],
        compiler_params=pltpu.CompilerParams(
            collective_id=0, has_side_effects=True, vmem_limit_bytes=58 << 20
        ),
    )(*flat, temporal_query, temporal_key, temporal_value)
    mixed, out = copy_out(mixed, out)
    return mixed.reshape(1, 1, 128, 3072), out.reshape(1, 8, 128, 384)


def solution(mesh):
    placed = (
        P("frame", "view", None, None),
        P("frame", "view", None, None),
        P("frame", "view", None, None),
        P("frame", "view", None, None),
        P("frame", None, None),
        P("frame", None, None),
        P(None, "view"),
        P(None, "view"),
        P(None, "view"),
    )
    return jax.shard_map(
        on_device,
        mesh=mesh,
        in_specs=placed,
        out_specs=(P("frame", "view", None, None), P("frame", None, None, "view")),
        check_vma=False,
    )
```
